128 devices in a mesh: row: 16 (over x_hi, y, core), col: 8 (over z, x_lo).
Axes of the slice: x: 4 (x_hi: 2, x_lo: 2; x = x_hi * 2 + x_lo), y: 4, z: 4, core: 2. Of those that a mesh axis runs over, the one named last changes fastest.
Arguments:
- children: bfloat16 [8, 16, 256, 8, 8, 256], P(None, 'row', None, None, 'col'), may hold values from -1 to 8193
- child_maps: int32 [2, 64], replicated, may hold values from 0 to 102, as said below
- coupling: bfloat16 [7, 16, 256, 1024], P(None, 'row'), may hold values from -48 to 48
- pivot_shift: float32 [1024], replicated, may hold values from 1280 to 2304
Outputs:
- factored_front: bfloat16 [7, 16, 256, 14, 8, 256], P(None, 'row', None, None, 'col')
The draws below stay inside these ranges and needn't reach their ends.
Inputs may be any that keep to these rules, and one draw needn't show every extreme that they name: Each child_maps[h] is strictly increasing. child_maps[0, t] = t for t < 4, and every other entry is 4 or more. For every h and every q < 8, at most 1 of the tiles child_maps[h, a * 8 + q] (a < 8) share a remainder modulo 2 * 8; for every c < 8, at most 1 of the tiles child_maps[h, b * 8 + c] (b < 8) share a remainder modulo 8. Both bounds are reached.
All inputs are finite; a program needn't handle non-finite values.
Results may differ from the reference program's by a relative error of at most 0.0048.
The reference program's roundings to bfloat16 on the way count: a program that leaves them out, or rounds other values in their place, can miss the bound.
Values may be sent and summed in bfloat16 or wider, within the bound.
No kernel may reach another device: no remote copies, remote signals or barrier semaphores. Data moves between devices by JAX's collectives and lax.ppermute only.
A program may use at most 192 MiB of HBM per device.

```python
import jax
import jax.numpy as jnp
from jax import lax

TILE = 256
NT = 112
NCT = 64
PANELS = 4
NP = 28672
PW = 1024
HALF = 8
RL = 7
CL = 14
CRL = 8
CCL = 8
N_ROW = 16
N_COL = 8


def draw_child_maps(key, part):
    key = jax.random.fold_in(key, 7)
    positions = jnp.arange(NCT, dtype=jnp.int32)
    listed = []
    for child_side in range(2):
        side_key = jax.random.fold_in(key, child_side)
        jump_at = jax.random.randint(side_key, (), PANELS, NCT)
        offset_base = child_side * 2 * HALF
        listed.append(positions + positions // HALF + offset_base + 2 * HALF * (positions >= jump_at).astype(jnp.int32))
    return jnp.stack(listed).astype(jnp.int32)


def draw_children(key, part):
    key = jax.random.fold_in(key, 11)
    noise_key = jax.random.fold_in(key, 0)
    weight_key = jax.random.fold_in(key, 2)
    order_key = jax.random.fold_in(key, 3)
    shape = (CRL, N_ROW, TILE, CCL, N_COL, TILE)
    noise = jax.random.uniform(noise_key, shape, jnp.float32, -1.0, 1.0)
    weights = jax.random.uniform(weight_key, (PW,), jnp.float32, 0.5, 2.0)
    weights = weights.at[0].set(2.0)
    order = jax.random.permutation(order_key, PW).astype(jnp.float32)
    distance = jnp.abs(order[:, None] - order[None, :])
    kernel = 2.0 * PW * weights[:, None] * weights[None, :] * jnp.exp(-distance / 4.0)
    kernel = kernel.reshape(PANELS, TILE, PANELS, TILE)
    noise = noise.at[0, :PANELS, :, 0, :PANELS, :].add(kernel)
    return noise.astype(jnp.bfloat16)


def block_levels(own_key, shape, pieces, smallest, largest):
    loudness, own = 1.0, jax.random.fold_in(own_key, 6)
    for axis_at, shards_of in pieces:
        heights = jnp.exp(jax.random.uniform(jax.random.fold_in(own, axis_at), (shards_of,), jnp.float32, smallest / len(pieces), largest / len(pieces)))
        loudness = loudness * jnp.repeat(heights, shape[axis_at] // shards_of).reshape([-1 if axis == axis_at else 1 for axis in range(len(shape))])
    return loudness


def bell_draw(key, shape, spread, most, pieces=(), kind=jnp.bfloat16):
    drawn = jax.random.normal(key, shape, jnp.float32) * spread
    if len(pieces) > 0:
        drawn = block_levels(key, shape, pieces, -0.22, 0.18) * drawn
    return jnp.clip(drawn, min=-most, max=most).astype(kind)


def setup_inputs(seed: int = 0) -> dict:
    splits = jax.random.split(jax.random.key(seed), 5)
    children = draw_children(jax.random.fold_in(splits[4], 71), 0)
    child_maps = draw_child_maps(jax.random.fold_in(splits[4], 71), 0)
    coupling = bell_draw(splits[2], (RL, N_ROW, TILE, PW), 8.0, 48.0, ((1, 16),))
    pivot_shift = jnp.clip(jax.random.uniform(splits[3], (PW,), jnp.float32, 1280.0, 2304.0), 1280.0, 2304.0)
    return dict(children=children, child_maps=child_maps, coupling=coupling, pivot_shift=pivot_shift)


def child_tiles(children, child_side):
    part_rows = children[:, child_side * HALF:(child_side + 1) * HALF]
    child_block = part_rows.reshape(NCT, TILE, NCT, TILE)
    return jnp.transpose(child_block, (0, 2, 1, 3)).astype(jnp.float32)

def reference(children, child_maps, coupling, pivot_shift):
    assembled = jnp.zeros((NT, NT, TILE, TILE), jnp.float32)
    for child_side in range(2):
        placed = child_maps[child_side].astype(jnp.int32)
        assembled = assembled.at[placed[:, None], placed[None, :]].add(child_tiles(children, child_side))
    pivot_strip = jnp.transpose(assembled[:, :PANELS], (0, 2, 1, 3)).reshape(NP, PW)
    row_number = jnp.arange(NP, dtype=jnp.int32)
    pivot_strip = pivot_strip + jnp.where(row_number[:, None] >= PW, coupling.reshape(NP, PW).astype(jnp.float32), 0.0)
    pivot_strip = pivot_strip.at[:PW].add(jnp.diag(pivot_shift))
    columns = []
    for panel_step in range(PANELS):
        start = panel_step * TILE
        corner = pivot_strip[start:start + TILE, start:start + TILE]
        symmetric = jnp.tril(corner) + jnp.transpose(jnp.tril(corner, -1))
        factor = jnp.linalg.cholesky(symmetric)
        below_rows = pivot_strip[start + TILE:, start:start + TILE]
        solved = jnp.transpose(jax.scipy.linalg.solve_triangular(factor, jnp.transpose(below_rows), lower=True))
        panel_cols = jnp.concatenate([jnp.zeros((start, TILE), jnp.float32), factor, solved], axis=0).astype(jnp.bfloat16)
        columns.append(panel_cols)
        if panel_step + 1 < PANELS:
            later = jnp.dot(panel_cols.astype(jnp.float32), jnp.transpose(panel_cols[start + TILE:PW]).astype(jnp.float32), preferred_element_type=jnp.float32)
            pivot_strip = pivot_strip.at[:, start + TILE:].add(-later)
    factor_cols = jnp.concatenate(columns, axis=1)
    trailing = jnp.transpose(factor_cols[PW:])

    def one_row(tile_index):
        tile_block = assembled[tile_index]
        row_values = jnp.transpose(tile_block, (1, 0, 2)).reshape(TILE, NP)[:, PW:]
        own_rows = lax.dynamic_slice_in_dim(factor_cols, tile_index * TILE, TILE, 0)
        schur_part = row_values - jnp.dot(own_rows.astype(jnp.float32), trailing.astype(jnp.float32), preferred_element_type=jnp.float32)
        schur_part = jnp.where(tile_index >= PANELS, schur_part, 0.0)
        return jnp.concatenate([own_rows, schur_part.astype(jnp.bfloat16)], axis=1)
    result_rows = lax.map(one_row, jnp.arange(NT, dtype=jnp.int32))
    return result_rows.reshape(RL, N_ROW, TILE, CL, N_COL, TILE)
```

```python
import functools

import jax
import jax.numpy as jnp
from jax import lax
from jax.experimental import pallas as pl
from jax.experimental.pallas import tpu as pltpu
from jax.sharding import Mesh, PartitionSpec as P

f32 = jnp.float32
bf16 = jnp.bfloat16
i32 = jnp.int32

T = 256
PANELS = 4
NB = 32
RL, CL = 7, 14
K = 7
VMEM = 56 * 1024 * 1024

ROW = ("xh", "y1", "y0", "core")
COL = ("z1", "z0", "xl")
ALL = ROW + COL
PLANE = ("y1", "y0", "core", "z1", "z0")
SPREAD = ("xh", "y1", "z1")
CHIPS = ("xh", "y1", "y0", "z1", "z0", "xl")


def permutation(move):
    pairs = []
    for row in range(16):
        for col in range(8):
            at = (row // 8, row // 2 % 4, row % 2, col // 2, col % 2)
            xh, y, core, z, xl = move(*at)
            pairs.append((row * 8 + col, (xh * 8 + y % 4 * 2 + core) * 8 + z % 4 * 2 + xl))
    return pairs


def exchange(x, axes):
    return lax.all_to_all(x, axes, split_axis=0, concat_axis=0, tiled=True)


def dot_t(a, b):
    return lax.dot_general(a, b, (((1,), (1,)), ((), ())), preferred_element_type=f32)


def split2(x):
    high = x.astype(bf16)
    return high, (x - high.astype(f32)).astype(bf16)


def split3(x):
    high = x.astype(bf16)
    rest = x - high.astype(f32)
    mid = rest.astype(bf16)
    return high, mid, (rest - mid.astype(f32)).astype(bf16)


def solve_t(x, inv_high, inv_low):
    high, low = split2(x)
    return dot_t(high, inv_high) + (dot_t(high, inv_low) + dot_t(low, inv_high))


def pack_kernel(s_ref, x_ref, *out_refs):
    rows = lax.broadcasted_iota(i32, (T, T), 0)
    cols = lax.broadcasted_iota(i32, (T, T), 1)
    pick = jnp.where((rows % 32) * 8 + rows // 32 == cols, 1.0, 0.0).astype(bf16)

    def group(g, _):
        part = x_ref[0, pl.ds(pl.multiple_of(g * T, T), T), :]
        moved = jnp.dot(pick, part, preferred_element_type=f32).astype(bf16)
        at = pl.ds(pl.multiple_of(g * 32, 32), 32)
        for b in range(8):
            for e in range(2):

                @pl.when(s_ref[16 + b] == e)
                def _():
                    out_refs[e][0, s_ref[8 + b], at, :] = moved[b * 32 : (b + 1) * 32]

        return 0

    lax.fori_loop(0, 8, group, 0)


def pack(scalars, tiles):
    shape = jax.ShapeDtypeStruct((8, 4, T, T), bf16)
    spec = pl.BlockSpec((1, 4, T, T), lambda a, s: (s[a], 0, 0, 0))
    return pl.pallas_call(
        pack_kernel,
        out_shape=(shape, shape),
        grid_spec=pltpu.PrefetchScalarGridSpec(
            num_scalar_prefetch=1,
            grid=(8,),
            in_specs=[pl.BlockSpec((1, 8 * T, T), lambda a, s: (a, 0, 0))],
            out_specs=[spec, spec],
        ),
        compiler_params=pltpu.CompilerParams(vmem_limit_bytes=VMEM),
        cost_estimate=pl.CostEstimate(flops=2 * 64 * T**3, bytes_accessed=1 << 24, transcendentals=0),
        name="pack",
    )(scalars, tiles)


def copy_kernel(s_ref, x_ref, out_ref):
    out_ref[...] = x_ref[...]


def compact(which, tiles):
    count = which.shape[0]
    return pl.pallas_call(
        copy_kernel,
        out_shape=jax.ShapeDtypeStruct((count, 4, T, T), bf16),
        grid_spec=pltpu.PrefetchScalarGridSpec(
            num_scalar_prefetch=1,
            grid=(count,),
            in_specs=[pl.BlockSpec((1, 4, T, T), lambda a, s: (s[a], 0, 0, 0))],
            out_specs=pl.BlockSpec((1, 4, T, T), lambda a, s: (a, 0, 0, 0)),
        ),
        compiler_params=pltpu.CompilerParams(vmem_limit_bytes=VMEM),
        cost_estimate=pl.CostEstimate(flops=0, bytes_accessed=count << 20, transcendentals=0),
        name="compact",
    )(which, tiles)


def factor_tile(aug):
    row_id = lax.broadcasted_iota(i32, (8, 128), 0)
    groups = NB // 8

    def block(step, _):
        at = pl.multiple_of(step * NB, NB)
        rows = [aug[pl.ds(pl.multiple_of(at + 8 * g, 8), 8), :] for g in range(groups)]
        back = lax.rem(T - at, T)
        diag = [pltpu.roll(rows[g][:, :T], back, 1)[:, :128] for g in range(groups)]
        scales = []
        for s in range(groups):
            cols = [
                [jnp.broadcast_to(diag[g][:, 8 * s + m : 8 * s + m + 1], (8, 128)) for g in range(s, groups)]
                for m in range(8)
            ]
            scale = jnp.zeros((8, 128), f32)
            for m in range(8):
                pivot = jnp.broadcast_to(cols[m][0][m : m + 1, :], (8, 128))
                inverse = 1.0 / pivot
                scale = jnp.where(row_id == m, lax.rsqrt(pivot), scale)
                factor = [c * inverse for c in cols[m]]
                factor[0] = jnp.where(row_id > m, factor[0], 0.0)
                for later in range(m + 1, 8):
                    value = jnp.broadcast_to(cols[later][0][m : m + 1, :], (8, 128))
                    cols[later] = [c - f * value for c, f in zip(cols[later], factor)]
                diag_row = jnp.broadcast_to(diag[s][m : m + 1, :], (8, 128))
                full_row = rows[s][m : m + 1, :]
                for g in range(s, groups):
                    f = factor[g - s]
                    diag[g] = diag[g] - f * diag_row
                    rows[g] = rows[g] - jnp.concatenate([f] * 4, axis=1) * full_row
            scales.append(scale)
        upper = jnp.concatenate(
            [rows[g] * jnp.concatenate([scales[g]] * 4, axis=1) for g in range(groups)], axis=0
        )
        aug[pl.ds(at, NB), :] = upper
        high, mid, low = split3(upper)
        keep = lax.broadcasted_iota(i32, (NB, T), 1) >= at + NB
        none = jnp.zeros((NB, T), bf16)
        lh, lm, ll = [jnp.where(keep, part[:, :T], none) for part in (high, mid, low)]
        left = jnp.concatenate([lh, lh, lm, lh, ll, lm], axis=0)
        right = jnp.concatenate([high, mid, high, low, high, mid], axis=0)
        aug[...] = aug[...] - lax.dot_general(
            left, right, (((0,), (0,)), ((), ())), preferred_element_type=f32
        )
        return 0

    lax.fori_loop(0, T // NB, block, 0)


def pivot_kernel(core_ref, own_ref, other_ref, shift_ref, lb_ref, high_ref, low_ref, work, aug):
    rows = lax.broadcasted_iota(i32, (T, T), 0)
    cols = lax.broadcasted_iota(i32, (T, T), 1)
    core = core_ref[0]
    for t in range(PANELS):
        for u in range(t + 1):
            for s in range(8):
                at = (((s // 2) * 2 + t // 2) * 2 + s % 2) * 4 + u
                part = jnp.where(core == t % 2, own_ref[at].astype(f32), other_ref[at].astype(f32))
                work[t, u, s * 32 : (s + 1) * 32, :] = part
        tile = jnp.where(rows >= cols, work[t, t], 0.0)
        work[t, t] = tile + jnp.where(rows == cols, 0.0, tile).T + jnp.where(rows == cols, shift_ref[t], 0.0)
    for k in range(PANELS):
        aug[:, :T] = work[k, k]
        aug[:, T:] = jnp.where(rows == cols, 1.0, 0.0)
        factor_tile(aug)
        lower = jnp.where(rows >= cols, aug[:, :T].T, 0.0)
        inv_high, inv_low = split2(aug[:, T:])
        high_ref[k] = inv_high
        low_ref[k] = inv_low
        for t in range(k):
            lb_ref[k, t * T : (t + 1) * T, :] = jnp.zeros((T, T), bf16)
        lb_ref[k, k * T : (k + 1) * T, :] = lower.astype(bf16)
        for t in range(k + 1, PANELS):
            lb_ref[k, t * T : (t + 1) * T, :] = solve_t(work[t, k], inv_high, inv_low).astype(bf16)
        for t in range(k + 1, PANELS):
            for u in range(k + 1, t + 1):
                work[t, u] = work[t, u] - dot_t(
                    lb_ref[k, t * T : (t + 1) * T, :], lb_ref[k, u * T : (u + 1) * T, :]
                )


def pivot(core, own, other, shift):
    vmem = pl.BlockSpec(memory_space=pltpu.VMEM)
    return pl.pallas_call(
        pivot_kernel,
        out_shape=(
            jax.ShapeDtypeStruct((PANELS, PANELS * T, T), bf16),
            jax.ShapeDtypeStruct((PANELS, T, T), bf16),
            jax.ShapeDtypeStruct((PANELS, T, T), bf16),
        ),
        in_specs=[pl.BlockSpec(memory_space=pltpu.SMEM), vmem, vmem, vmem],
        out_specs=[vmem] * 3,
        scratch_shapes=[pltpu.VMEM((PANELS, PANELS, T, T), f32), pltpu.VMEM((T, 2 * T), f32)],
        compiler_params=pltpu.CompilerParams(vmem_limit_bytes=VMEM),
        cost_estimate=pl.CostEstimate(flops=45_000_000_000, bytes_accessed=1 << 22, transcendentals=0),
        name="pivot_factor",
    )(core, own, other, shift)


def panel_kernel(s_ref, strip_ref, coupling_ref, lb_ref, high_ref, low_ref, out_ref):
    a = pl.program_id(0)
    row = s_ref[14]
    found = s_ref[7 + a].astype(f32)
    done = []
    for k in range(PANELS):
        block = strip_ref[:, 0, k].reshape(T, T).astype(f32) * found
        block = block + coupling_ref[0, :, k * T : (k + 1) * T].astype(f32)
        for j in range(k):
            block = block - dot_t(done[j], lb_ref[j, k * T : (k + 1) * T, :])
        solved = solve_t(block, high_ref[k], low_ref[k]).astype(bf16)
        done.append(solved)
        out_ref[0, :, k * T : (k + 1) * T] = solved

    @pl.when((a == 0) & (row < PANELS))
    def _():
        at = pl.ds(pl.multiple_of(row * T, T), T)
        for k in range(PANELS):
            out_ref[0, :, k * T : (k + 1) * T] = lb_ref[k, at, :]


def panel_rows(scalars, strip, coupling, lb, high, low):
    whole = lambda shape: pl.BlockSpec(shape, lambda a, s: (0,) * len(shape))
    return pl.pallas_call(
        panel_kernel,
        out_shape=jax.ShapeDtypeStruct((RL, T, PANELS * T), bf16),
        grid_spec=pltpu.PrefetchScalarGridSpec(
            num_scalar_prefetch=1,
            grid=(RL,),
            in_specs=[
                pl.BlockSpec((8, 1, PANELS, 32, T), lambda a, s: (0, s[a], 0, 0, 0)),
                pl.BlockSpec((1, T, PANELS * T), lambda a, s: (a, 0, 0)),
                whole((PANELS, PANELS * T, T)),
                whole((PANELS, T, T)),
                whole((PANELS, T, T)),
            ],
            out_specs=pl.BlockSpec((1, T, PANELS * T), lambda a, s: (a, 0, 0)),
        ),
        compiler_params=pltpu.CompilerParams(vmem_limit_bytes=VMEM),
        cost_estimate=pl.CostEstimate(flops=8_000_000_000, bytes_accessed=12 << 20, transcendentals=0),
        name="panel_rows",
    )(scalars, strip, coupling, lb, high, low)


PIECES = ((0, 2), (2, 4), (4, 6), (6, 7))


def front_kernel(s_ref, rows_ref, *refs):
    blocks = refs[0:4]
    own, other = refs[4:8], refs[8:12]
    out_ref = refs[12]
    a = pl.program_id(0)
    row, col, core = s_ref[119], s_ref[120], s_ref[121]
    row_ok = [s_ref[21 + a], s_ref[28 + a]]
    mine = rows_ref[0]
    for j, (lo, hi) in enumerate(PIECES):
        for held, parity in ((own[j], core), (other[j], 1 - core)):
            for n in range(hi - lo):
                b = 2 * (lo + n) + parity
                tile = -dot_t(mine, held[n])
                for f in range(2):
                    base = 35 + 42 * f
                    z, e = s_ref[base + b], s_ref[base + 14 + b]
                    ok = row_ok[f] * s_ref[base + 28 + b]
                    at0 = (ok * (1 - e)).astype(f32)
                    at1 = (ok * e).astype(f32)
                    tile = tile + blocks[2 * f][0, z].astype(f32) * at0
                    tile = tile + blocks[2 * f + 1][0, z].astype(f32) * at1
                out_ref[0, b] = tile.astype(bf16)

    @pl.when((a == 0) & (row < PANELS))
    def _():
        out_ref[...] = jnp.zeros_like(out_ref)

    @pl.when(col < PANELS)
    def _():
        out_ref[0, 0] = rows_ref[0, :, pl.ds(pl.multiple_of(jnp.minimum(col, PANELS - 1) * T, T), T)]


def front(scalars, rows, blocks, own, other):
    block = lambda first: pl.BlockSpec((1, 4, T, T), lambda a, s: (s[first + a], 0, 0, 0))
    whole = lambda x: pl.BlockSpec(x.shape, lambda a, s: (0, 0, 0))
    return pl.pallas_call(
        front_kernel,
        out_shape=jax.ShapeDtypeStruct((RL, CL, T, T), bf16),
        grid_spec=pltpu.PrefetchScalarGridSpec(
            num_scalar_prefetch=1,
            grid=(RL,),
            in_specs=[
                pl.BlockSpec((1, T, PANELS * T), lambda a, s: (a, 0, 0)),
                block(0),
                block(7),
                block(14),
                block(14),
            ]
            + [whole(x) for x in own]
            + [whole(x) for x in other],
            out_specs=pl.BlockSpec((1, CL, T, T), lambda a, s: (a, 0, 0, 0)),
        ),
        compiler_params=pltpu.CompilerParams(vmem_limit_bytes=VMEM),
        cost_estimate=pl.CostEstimate(
            flops=2 * RL * CL * T * T * PANELS * T, bytes_accessed=40 << 20, transcendentals=0
        ),
        name="front",
    )(scalars, rows, *blocks, *own, *other)


def per_device(children, child_maps, coupling, pivot_shift):
    row, col = lax.axis_index(ROW), lax.axis_index(COL)
    xh, core, xl = lax.axis_index("xh"), lax.axis_index("core"), lax.axis_index("xl")
    rho = row % 8
    eight = jnp.arange(8)

    own_map = child_maps[xh].reshape(8, 8)
    row_to = jnp.sum(jnp.where(eight[None, :] == rho, own_map, 0), axis=1)
    col_to = jnp.sum(jnp.where(eight[None, :] == col, own_map, 0), axis=1)
    pack_scalars = jnp.concatenate([row_to % 8, col_to % 8 // 2, (col_to % 2) ^ xl]).astype(i32)

    tiles = children.reshape(8, T, 8, T)

    first = tiles[0, :, 0, :].reshape(8, 32, T)
    piece = exchange(first, SPREAD)[0]
    own_half = exchange(jnp.broadcast_to(piece[None], (64, 32, T)), CHIPS)
    swap = permutation(lambda xh, y, core, z, xl: (xh, y, 1 - core, z, xl))
    other_half = lax.ppermute(own_half, ALL, swap)

    sixteen = jnp.arange(16)
    from_a = jnp.sum(jnp.where(row_to[None, :] % 16 == sixteen[:, None], eight[None, :], 0), axis=1)
    strip = tiles[:, :, 0, :].reshape(8, 8, 32, T)[from_a].reshape(128, 32, T)
    strip = exchange(strip, ALL).reshape(16, 8, 32, T)[:8, :PANELS]
    strip = exchange(jnp.broadcast_to(strip[None], (8, 8, PANELS, 32, T)), COL)

    lb, high, low = pivot(core.reshape(1), own_half, other_half, pivot_shift.reshape(PANELS, T, 1))

    both = jnp.stack([child_maps[xh], child_maps[1 - xh]])
    at = jnp.arange(64)
    row_is = both[:, None, :] == (row + 16 * jnp.arange(RL))[None, :, None]
    row_t = jnp.sum(jnp.where(row_is, at, 0), axis=2)
    row_ok = jnp.any(row_is, axis=2).astype(i32)
    col_is = both[:, None, :] == (col + 8 * jnp.arange(CL))[None, :, None]
    col_u = jnp.sum(jnp.where(col_is, at, 0), axis=2)
    col_ok = jnp.any(col_is, axis=2).astype(i32)
    by_q = both.reshape(2, 8, 8)
    half = jnp.sum(jnp.where(by_q % 8 == rho, by_q // 8 % 2, 0), axis=1)
    rank_of = lambda hit: jnp.sum(
        jnp.where(eight[None, :] < eight[:, None], hit[..., None, :].astype(i32), 0), axis=-1
    )
    rank = rank_of(half == xh)
    slot = jnp.sum(jnp.where(row_t[:, :, None] % 8 == eight, rank[:, None, :], 0), axis=2) * row_ok

    def chosen(hit):
        order = jnp.where(hit[None, :] & (rank_of(hit)[None, :] == jnp.arange(K)[:, None]), eight[None, :], 0)
        return jnp.sum(order, axis=1).astype(i32)

    to_own, to_other = chosen(half[0] == xh), chosen(half[0] != xh)

    zero_is = child_maps[0][None, :] == (row + 16 * jnp.arange(RL))[:, None]
    panel_scalars = jnp.concatenate(
        [
            jnp.sum(jnp.where(zero_is, at % 8, 0), axis=1),
            jnp.any(zero_is, axis=1).astype(i32),
            row.reshape(1),
        ]
    ).astype(i32)
    front_scalars = jnp.concatenate(
        [row_t[0] % 8, slot[0], slot[1], row_ok[0], row_ok[1]]
        + [x[f] for f in range(2) for x in (col_u % 8 // 2, (col_u % 2) ^ xl, col_ok)]
        + [row.reshape(1), col.reshape(1), core.reshape(1)]
    ).astype(i32)

    packed_same, packed_cross = pack(pack_scalars, children.reshape(8, 8 * T, T))
    cross = exchange(packed_cross.reshape(32, T, T), PLANE).reshape(8, 4, T, T)
    same = exchange(packed_same.reshape(32, T, T), PLANE).reshape(8, 4, T, T)
    move = lambda f, e: permutation(lambda xh, y, core, z, xl: (xh ^ f, y, core, z, xl ^ e))
    from_01 = lax.ppermute(compact(to_own, cross), ALL, move(0, 1))
    from_11 = lax.ppermute(compact(to_other, cross), ALL, move(1, 1))
    from_10 = lax.ppermute(compact(to_other, same), ALL, move(1, 0))

    rows = panel_rows(panel_scalars, strip, coupling.reshape(RL, T, PANELS * T), lb, high, low)

    own, other = [], []
    for j, (lo, hi) in enumerate(PIECES):
        turn = permutation(lambda xh, y, core, z, xl: (xl ^ (j % 2), z - y + j, xh, y, core))
        own.append(lax.ppermute(rows[lo:hi], ALL, turn))
        other.append(lax.ppermute(own[-1], ALL, swap))

    result = front(front_scalars, rows, (same, from_01, from_10, from_11), own, other)
    return jnp.transpose(result, (0, 2, 1, 3)).reshape(RL, 1, T, CL, 1, T)


def solution(mesh):
    fine = Mesh(mesh.devices.reshape((2,) * 7), ALL)
    in_specs = (P(None, ROW, None, None, COL, None), P(), P(None, ROW, None, None), P())
    out_specs = P(None, ROW, None, None, COL, None)
    return jax.shard_map(per_device, mesh=fine, in_specs=in_specs, out_specs=out_specs, check_vma=False)
```

```python
import jax
import jax.numpy as jnp
from jax import lax
from jax.experimental import pallas as pl
from jax.experimental.pallas import tpu as pltpu
from jax.sharding import Mesh, PartitionSpec as P

f32 = jnp.float32
bf16 = jnp.bfloat16
i32 = jnp.int32

T = 256
PANELS = 4
NB = 32
RL, CL = 7, 14
K = 7
FIRST = 5
VMEM = 56 * 1024 * 1024

ROW = ("xh", "y1", "y0", "core")
COL = ("z1", "z0", "xl")
ALL = ROW + COL
PLANE = ("y1", "y0", "core", "z1", "z0")
CHIPS = ("xh", "y1", "y0", "z1", "z0", "xl")


def permutation(move):
    pairs = []
    for row in range(16):
        for col in range(8):
            at = (row // 8, row // 2 % 4, row % 2, col // 2, col % 2)
            xh, y, core, z, xl = move(*at)
            pairs.append((row * 8 + col, (xh * 8 + y % 4 * 2 + core) * 8 + z % 4 * 2 + xl))
    return pairs


def exchange(x, axes):
    return lax.all_to_all(x, axes, split_axis=0, concat_axis=0, tiled=True)


def dot_t(a, b):
    return lax.dot_general(a, b, (((1,), (1,)), ((), ())), preferred_element_type=f32)


def split2(x):
    high = x.astype(bf16)
    return high, (x - high.astype(f32)).astype(bf16)


def split3(x):
    high = x.astype(bf16)
    rest = x - high.astype(f32)
    mid = rest.astype(bf16)
    return high, mid, (rest - mid.astype(f32)).astype(bf16)


def solve_t(x, inv_high, inv_low):
    high, low = split2(x)
    return dot_t(high, inv_high) + (dot_t(high, inv_low) + dot_t(low, inv_high))


def pack_kernel(s_ref, x_ref, same_ref, cross_ref, strip_ref, first_ref, moved):
    rows = lax.broadcasted_iota(i32, (T, T), 0)
    cols = lax.broadcasted_iota(i32, (T, T), 1)
    pick = jnp.where((rows % 32) * 8 + rows // 32 == cols, 1.0, 0.0).astype(bf16)
    for g in range(8):
        part = x_ref[0, g * T : (g + 1) * T, :]
        tiles = jnp.dot(pick, part, preferred_element_type=f32).astype(bf16)
        moved[g % 2] = tiles
        strip_ref[0, g] = tiles[:32]
        for e, out_ref in enumerate((same_ref, cross_ref)):
            for z in range(4):
                at = pl.ds(pl.multiple_of(s_ref[16 + 4 * e + z] * 32, 32), 32)
                out_ref[0, z, g * 32 : (g + 1) * 32, :] = moved[g % 2, at, :]

    @pl.when(pl.program_id(0) == 0)
    def _():
        first_ref[...] = strip_ref[0]


def pack(scalars, tiles):
    shape = jax.ShapeDtypeStruct((8, 4, T, T), bf16)
    spec = pl.BlockSpec((1, 4, T, T), lambda a, s: (s[a], 0, 0, 0))
    return pl.pallas_call(
        pack_kernel,
        out_shape=(
            shape,
            shape,
            jax.ShapeDtypeStruct((16, 8, 32, T), bf16),
            jax.ShapeDtypeStruct((8, 32, T), bf16),
        ),
        grid_spec=pltpu.PrefetchScalarGridSpec(
            num_scalar_prefetch=1,
            grid=(8,),
            in_specs=[pl.BlockSpec((1, 8 * T, T), lambda a, s: (a, 0, 0))],
            out_specs=[
                spec,
                spec,
                pl.BlockSpec((1, 8, 32, T), lambda a, s: (s[8 + a], 0, 0, 0)),
                pl.BlockSpec((8, 32, T), lambda a, s: (0, 0, 0)),
            ],
            scratch_shapes=[pltpu.VMEM((2, T, T), bf16)],
        ),
        compiler_params=pltpu.CompilerParams(vmem_limit_bytes=VMEM),
        cost_estimate=pl.CostEstimate(flops=2 * 64 * T**3, bytes_accessed=1 << 24, transcendentals=0),
        name="pack",
    )(scalars, tiles)


def copy_kernel(s_ref, *refs):
    half = len(refs) // 2
    for x_ref, out_ref in zip(refs[:half], refs[half:]):
        out_ref[...] = x_ref[...]


def compact(lists, tiles):
    count = lists[0].shape[0]
    block = lambda n: pl.BlockSpec((1, 4, T, T), lambda a, s: (s[n * count + a], 0, 0, 0))
    return pl.pallas_call(
        copy_kernel,
        out_shape=[jax.ShapeDtypeStruct((count, 4, T, T), bf16) for _ in lists],
        grid_spec=pltpu.PrefetchScalarGridSpec(
            num_scalar_prefetch=1,
            grid=(count,),
            in_specs=[block(n) for n in range(len(lists))],
            out_specs=[pl.BlockSpec((1, 4, T, T), lambda a, s: (a, 0, 0, 0)) for _ in lists],
        ),
        compiler_params=pltpu.CompilerParams(vmem_limit_bytes=VMEM),
        cost_estimate=pl.CostEstimate(flops=0, bytes_accessed=len(lists) * count << 20, transcendentals=0),
        name="compact",
    )(jnp.concatenate(lists), *[tiles for _ in lists])


def factor_tile(aug):
    row_id = lax.broadcasted_iota(i32, (8, 128), 0)
    groups = NB // 8

    def block(step, _):
        at = pl.multiple_of(step * NB, NB)
        rows = [aug[pl.ds(pl.multiple_of(at + 8 * g, 8), 8), :] for g in range(groups)]
        back = lax.rem(T - at, T)
        diag = [pltpu.roll(rows[g][:, :T], back, 1)[:, :128] for g in range(groups)]
        scales = []
        for s in range(groups):
            cols = [
                [jnp.broadcast_to(diag[g][:, 8 * s + m : 8 * s + m + 1], (8, 128)) for g in range(s, groups)]
                for m in range(8)
            ]
            scale = jnp.zeros((8, 128), f32)
            for m in range(8):
                pivot = jnp.broadcast_to(cols[m][0][m : m + 1, :], (8, 128))
                inverse = 1.0 / pivot
                scale = jnp.where(row_id == m, lax.rsqrt(pivot), scale)
                factor = [c * inverse for c in cols[m]]
                factor[0] = jnp.where(row_id > m, factor[0], 0.0)
                for later in range(m + 1, 8):
                    value = jnp.broadcast_to(cols[later][0][m : m + 1, :], (8, 128))
                    cols[later] = [c - f * value for c, f in zip(cols[later], factor)]
                diag_row = jnp.broadcast_to(diag[s][m : m + 1, :], (8, 128))
                full_row = rows[s][m : m + 1, :]
                for g in range(s, groups):
                    f = factor[g - s]
                    diag[g] = diag[g] - f * diag_row
                    rows[g] = rows[g] - jnp.concatenate([f] * 4, axis=1) * full_row
            scales.append(scale)
        upper = jnp.concatenate(
            [rows[g] * jnp.concatenate([scales[g]] * 4, axis=1) for g in range(groups)], axis=0
        )
        aug[pl.ds(at, NB), :] = upper
        high, mid, low = split3(upper)
        keep = lax.broadcasted_iota(i32, (NB, T), 1) >= at + NB
        none = jnp.zeros((NB, T), bf16)
        lh, lm, ll = [jnp.where(keep, part[:, :T], none) for part in (high, mid, low)]
        left = jnp.concatenate([lh, lh, lm, lh, ll, lm], axis=0)
        right = jnp.concatenate([high, mid, high, low, high, mid], axis=0)
        aug[...] = aug[...] - lax.dot_general(
            left, right, (((0,), (0,)), ((), ())), preferred_element_type=f32
        )
        return 0

    lax.fori_loop(0, T // NB, block, 0)


def pivot_kernel(core_ref, own_ref, other_ref, shift_ref, lb_ref, high_ref, low_ref, work, aug):
    rows = lax.broadcasted_iota(i32, (T, T), 0)
    cols = lax.broadcasted_iota(i32, (T, T), 1)
    core = core_ref[0]
    for t in range(PANELS):
        for u in range(t + 1):
            for s in range(8):
                at = (((s // 2) * 2 + t // 2) * 2 + s % 2) * 4 + u
                part = jnp.where(core == t % 2, own_ref[at].astype(f32), other_ref[at].astype(f32))
                work[t, u, s * 32 : (s + 1) * 32, :] = part
        tile = jnp.where(rows >= cols, work[t, t], 0.0)
        work[t, t] = tile + jnp.where(rows == cols, 0.0, tile).T + jnp.where(rows == cols, shift_ref[t], 0.0)
    for k in range(PANELS):
        aug[:, :T] = work[k, k]
        aug[:, T:] = jnp.where(rows == cols, 1.0, 0.0)
        factor_tile(aug)
        lower = jnp.where(rows >= cols, aug[:, :T].T, 0.0)
        inv_high, inv_low = split2(aug[:, T:])
        high_ref[k] = inv_high
        low_ref[k] = inv_low
        for t in range(k):
            lb_ref[k, t * T : (t + 1) * T, :] = jnp.zeros((T, T), bf16)
        lb_ref[k, k * T : (k + 1) * T, :] = lower.astype(bf16)
        for t in range(k + 1, PANELS):
            lb_ref[k, t * T : (t + 1) * T, :] = solve_t(work[t, k], inv_high, inv_low).astype(bf16)
        for t in range(k + 1, PANELS):
            for u in range(k + 1, t + 1):
                work[t, u] = work[t, u] - dot_t(
                    lb_ref[k, t * T : (t + 1) * T, :], lb_ref[k, u * T : (u + 1) * T, :]
                )


def pivot(core, own, other, shift):
    vmem = pl.BlockSpec(memory_space=pltpu.VMEM)
    return pl.pallas_call(
        pivot_kernel,
        out_shape=(
            jax.ShapeDtypeStruct((PANELS, PANELS * T, T), bf16),
            jax.ShapeDtypeStruct((PANELS, T, T), bf16),
            jax.ShapeDtypeStruct((PANELS, T, T), bf16),
        ),
        in_specs=[pl.BlockSpec(memory_space=pltpu.SMEM), vmem, vmem, vmem],
        out_specs=[vmem] * 3,
        scratch_shapes=[pltpu.VMEM((PANELS, PANELS, T, T), f32), pltpu.VMEM((T, 2 * T), f32)],
        compiler_params=pltpu.CompilerParams(vmem_limit_bytes=VMEM),
        cost_estimate=pl.CostEstimate(flops=45_000_000_000, bytes_accessed=1 << 22, transcendentals=0),
        name="pivot_factor",
    )(core, own, other, shift)


PIECES = ((0, 4), (4, 7))


def panel_kernel(s_ref, *refs):
    strips, (coupling_ref, lb_ref, high_ref, low_ref) = refs[:2], refs[2:6]
    *outs, all_ref, done, block = refs[6:]
    k = pl.program_id(0)
    row, col = s_ref[14], s_ref[15]
    for a in range(RL):
        q = s_ref[a]
        for d in range(8):
            at = pl.ds(pl.multiple_of(a * T + (col ^ d) * 32, 32), 32)
            held = jnp.where(s_ref[7 + a] == 1, strips[d % 2][d // 2, q, 0].astype(f32), 0.0)
            block[at, :] = held
        at = slice(a * T, (a + 1) * T)
        block[at, :] = block[at, :] + coupling_ref[a].astype(f32)
    for j in range(PANELS - 1):

        @pl.when(j < k)
        def _():
            block[...] = block[...] - dot_t(done[j], lb_ref[j, pl.ds(pl.multiple_of(k * T, T), T), :])

    solved = solve_t(block[...], high_ref[k], low_ref[k]).astype(bf16)
    done[k] = solved
    all_ref[...] = solved.reshape(RL, T, T)
    for j, (lo, hi) in enumerate(PIECES):
        outs[j][...] = solved[lo * T : hi * T].reshape(hi - lo, T, T)

    @pl.when(row < PANELS)
    def _():
        pivot_rows = lb_ref[k, pl.ds(pl.multiple_of(jnp.minimum(row, PANELS - 1) * T, T), T), :]
        outs[0][0] = pivot_rows
        all_ref[0] = pivot_rows


def panel_rows(scalars, strips, coupling, lb, high, low):
    whole = lambda shape: pl.BlockSpec(shape, lambda k, s: (0,) * len(shape))
    return pl.pallas_call(
        panel_kernel,
        out_shape=[jax.ShapeDtypeStruct((hi - lo, T, PANELS * T), bf16) for lo, hi in (*PIECES, (0, RL))],
        grid_spec=pltpu.PrefetchScalarGridSpec(
            num_scalar_prefetch=1,
            grid=(PANELS,),
            in_specs=[pl.BlockSpec((4, 8, 1, 32, T), lambda k, s: (0, 0, k, 0, 0))] * 2
            + [
                pl.BlockSpec((RL, T, T), lambda k, s: (0, 0, k)),
                whole((PANELS, PANELS * T, T)),
                whole((PANELS, T, T)),
                whole((PANELS, T, T)),
            ],
            out_specs=[pl.BlockSpec((hi - lo, T, T), lambda k, s: (0, 0, k)) for lo, hi in (*PIECES, (0, RL))],
            scratch_shapes=[pltpu.VMEM((PANELS, RL * T, T), bf16), pltpu.VMEM((RL * T, T), f32)],
        ),
        compiler_params=pltpu.CompilerParams(vmem_limit_bytes=VMEM),
        cost_estimate=pl.CostEstimate(flops=8_000_000_000, bytes_accessed=12 << 20, transcendentals=0),
        name="panel_rows",
    )(scalars, *strips, coupling, lb, high, low)


def front_kernel(s_ref, rows_ref, *refs):
    blocks = refs[0:4]
    count = len(PIECES)
    own, other, out_ref = refs[4 : 4 + count], refs[4 + count : 4 + 2 * count], refs[-1]
    a = pl.program_id(0)
    row, col, core = s_ref[119], s_ref[120], s_ref[121]
    row_ok = [s_ref[21 + a], s_ref[28 + a]]
    mine = rows_ref[0]
    for j, (lo, hi) in enumerate(PIECES):
        for held, parity in ((own[j], core), (other[j], 1 - core)):
            for n in range(hi - lo):
                b = 2 * (lo + n) + parity
                tile = -dot_t(mine, held[n])
                for f in range(2):
                    base = 35 + 42 * f
                    z, e = s_ref[base + b], s_ref[base + 14 + b]
                    ok = row_ok[f] * s_ref[base + 28 + b]
                    near, far = blocks[2 * f][0, z].astype(f32), blocks[2 * f + 1][0, z].astype(f32)
                    tile = tile + jnp.where(e == 0, near, far) * ok.astype(f32)
                out_ref[0, b] = tile.astype(bf16)

    @pl.when((a == 0) & (row < PANELS))
    def _():
        out_ref[...] = jnp.zeros_like(out_ref)

    @pl.when(col < PANELS)
    def _():
        out_ref[0, 0] = rows_ref[0, :, pl.ds(pl.multiple_of(jnp.minimum(col, PANELS - 1) * T, T), T)]


def front(scalars, rows, blocks, own, other):
    block = lambda first: pl.BlockSpec((1, 4, T, T), lambda a, s: (s[first + a], 0, 0, 0))
    whole = lambda x: pl.BlockSpec(x.shape, lambda a, s: (0, 0, 0))
    return pl.pallas_call(
        front_kernel,
        out_shape=jax.ShapeDtypeStruct((RL, CL, T, T), bf16),
        grid_spec=pltpu.PrefetchScalarGridSpec(
            num_scalar_prefetch=1,
            grid=(RL,),
            in_specs=[
                pl.BlockSpec((1, T, PANELS * T), lambda a, s: (a, 0, 0)),
                block(0),
                block(7),
                block(14),
                block(14),
            ]
            + [whole(x) for x in own]
            + [whole(x) for x in other],
            out_specs=pl.BlockSpec((1, CL, T, T), lambda a, s: (a, 0, 0, 0)),
        ),
        compiler_params=pltpu.CompilerParams(vmem_limit_bytes=VMEM),
        cost_estimate=pl.CostEstimate(
            flops=2 * RL * CL * T * T * PANELS * T, bytes_accessed=40 << 20, transcendentals=0
        ),
        name="front",
    )(scalars, rows, *blocks, *own, *other)


def per_device(children, child_maps, coupling, pivot_shift):
    row, col = lax.axis_index(ROW), lax.axis_index(COL)
    xh, core, xl = lax.axis_index("xh"), lax.axis_index("core"), lax.axis_index("xl")
    rho = row % 8
    eight = jnp.arange(8)

    own_map = child_maps[xh].reshape(8, 8)
    row_to = jnp.sum(jnp.where(eight[None, :] == rho, own_map, 0), axis=1)
    col_to = jnp.sum(jnp.where(eight[None, :] == col, own_map, 0), axis=1)
    by_to = lambda slots: jnp.sum(jnp.where(col_to[None, :] % 8 == slots[:, None], eight[None, :], 0), axis=1)
    same_to = 2 * jnp.arange(4) + xl
    pack_scalars = jnp.concatenate(
        [row_to % 8, row_to % 16, by_to(same_to), by_to(same_to ^ 1)]
    ).astype(i32)

    both = jnp.stack([child_maps[xh], child_maps[1 - xh]])
    at = jnp.arange(64)
    row_is = both[:, None, :] == (row + 16 * jnp.arange(RL))[None, :, None]
    row_t = jnp.sum(jnp.where(row_is, at, 0), axis=2)
    row_ok = jnp.any(row_is, axis=2).astype(i32)
    col_is = both[:, None, :] == (col + 8 * jnp.arange(CL))[None, :, None]
    col_u = jnp.sum(jnp.where(col_is, at, 0), axis=2)
    col_ok = jnp.any(col_is, axis=2).astype(i32)
    by_q = both.reshape(2, 8, 8)
    half = jnp.sum(jnp.where(by_q % 8 == rho, by_q // 8 % 2, 0), axis=1)
    rank_of = lambda hit: jnp.sum(
        jnp.where(eight[None, :] < eight[:, None], hit[..., None, :].astype(i32), 0), axis=-1
    )
    rank = rank_of(half == xh)
    slot = jnp.sum(jnp.where(row_t[:, :, None] % 8 == eight, rank[:, None, :], 0), axis=2) * row_ok

    def chosen(hit):
        order = jnp.where(hit[None, :] & (rank_of(hit)[None, :] == jnp.arange(K)[:, None]), eight[None, :], 0)
        return jnp.sum(order, axis=1).astype(i32)

    to_own, to_other = chosen(half[0] == xh), chosen(half[0] != xh)

    zero_is = child_maps[0][None, :] == (row + 16 * jnp.arange(RL))[:, None]
    panel_scalars = jnp.concatenate(
        [
            jnp.sum(jnp.where(zero_is, at % 8, 0), axis=1),
            jnp.any(zero_is, axis=1).astype(i32),
            row.reshape(1),
            col.reshape(1),
        ]
    ).astype(i32)
    front_scalars = jnp.concatenate(
        [row_t[0] % 8, slot[0], slot[1], row_ok[0], row_ok[1]]
        + [x[f] for f in range(2) for x in (col_u % 8 // 2, (col_u % 2) ^ xl, col_ok)]
        + [row.reshape(1), col.reshape(1), core.reshape(1)]
    ).astype(i32)

    tiles = children.reshape(8, 8 * T, T)
    same, cross, strip, first = pack(pack_scalars, tiles)

    move = lambda f, e: permutation(lambda xh, y, core, z, xl: (xh ^ f, y, core, z, xl ^ e))
    swap = permutation(lambda xh, y, core, z, xl: (xh, y, 1 - core, z, xl))
    flip = lambda d: permutation(lambda xh, y, core, z, xl: (xh, y, core, z ^ (d // 2), xl ^ (d % 2)))
    cross = exchange(cross.reshape(32, T, T), PLANE).reshape(8, 4, T, T)
    strip, cross = lax.optimization_barrier((strip, cross))

    strip = exchange(strip.reshape(128, 32, T), ALL)
    send_01, send_11 = compact((to_own[:FIRST], to_other[:FIRST]), cross)

    piece = first[0]
    for s in range(1, 8):
        pairs = []
        for owner in range(16):
            t, u = owner // 4, owner % 4
            pairs.append((t * 8 + u, (t + s // 2 * 4) * 8 + u + s % 2 * 4))
        arrived = lax.ppermute(first[s], ALL, pairs)
        piece = jnp.where(row // 4 * 2 + col // 4 == s, arrived, piece)
    mine = strip.reshape(16, 8, 32, T)[:8, :PANELS]
    held = [mine] + [lax.ppermute(mine, ALL, flip(2 * d)) for d in range(1, 4)]
    piece, held, send_01, send_11 = lax.optimization_barrier((piece, held, send_01, send_11))
    own_half = exchange(jnp.broadcast_to(piece[None], (64, 32, T)), CHIPS)
    other_half = lax.ppermute(own_half, ALL, swap)
    same, held, other_half, send_01, send_11 = lax.optimization_barrier(
        (same, held, other_half, send_01, send_11)
    )

    held = jnp.stack(held)
    strips = [held, lax.ppermute(held, ALL, flip(1))]
    from_01 = lax.ppermute(send_01, ALL, move(0, 1))
    from_11 = lax.ppermute(send_11, ALL, move(1, 1))
    same = exchange(same.reshape(32, T, T), PLANE).reshape(8, 4, T, T)

    lb, high, low = pivot(core.reshape(1), own_half, other_half, pivot_shift.reshape(PANELS, T, 1))
    *rows, all_rows = panel_rows(panel_scalars, strips, coupling.reshape(RL, T, PANELS * T), lb, high, low)

    own, other = [], []
    for j in range(len(PIECES)):
        turn = permutation(lambda xh, y, core, z, xl: (xl ^ core ^ xh, z - y + j, xh, y, core))
        own.append(lax.ppermute(rows[j], ALL, turn))
        other.append(lax.ppermute(own[-1], ALL, swap))

    same, from_01, from_11, all_rows = lax.optimization_barrier((same, from_01, from_11, all_rows))
    from_10 = lax.ppermute(compact((to_other[:FIRST],), same)[0], ALL, move(1, 0))

    def finish(f01, f10, f11):
        return front(front_scalars, all_rows, (same, f01, f10, f11), own, other)

    def finish_rest(f01, f10, f11):
        rest_01, rest_11 = compact((to_own[FIRST:], to_other[FIRST:]), cross)
        rest_10 = compact((to_other[FIRST:],), same)[0]
        rest_01 = lax.ppermute(rest_01, ALL, move(0, 1))
        rest_11 = lax.ppermute(rest_11, ALL, move(1, 1))
        rest_10 = lax.ppermute(rest_10, ALL, move(1, 0))
        joined = [jnp.concatenate(pair) for pair in ((f01, rest_01), (f10, rest_10), (f11, rest_11))]
        return finish(*joined)

    ones = child_maps[:, None, :] % 16 == jnp.arange(16)[None, :, None]
    most = jnp.max(jnp.sum(ones.astype(i32), axis=2))
    result = lax.cond(most <= FIRST, finish, finish_rest, from_01, from_10, from_11)
    return jnp.transpose(result, (0, 2, 1, 3)).reshape(RL, 1, T, CL, 1, T)


def solution(mesh):
    fine = Mesh(mesh.devices.reshape((2,) * 7), ALL)
    in_specs = (P(None, ROW, None, None, COL, None), P(), P(None, ROW, None, None), P())
    out_specs = P(None, ROW, None, None, COL, None)
    return jax.shard_map(per_device, mesh=fine, in_specs=in_specs, out_specs=out_specs, check_vma=False)
```

```python
import jax
import jax.numpy as jnp
from jax import lax
from jax.experimental import pallas as pl
from jax.experimental.pallas import tpu as pltpu
from jax.sharding import Mesh, PartitionSpec as P

f32 = jnp.float32
bf16 = jnp.bfloat16
i32 = jnp.int32

T = 256
PANELS = 4
NB = 32
RL, CL = 7, 14
K = 7
FIRST = 5
VMEM = 56 * 1024 * 1024

ROW = ("xh", "y1", "y0", "core")
COL = ("z1", "z0", "xl")
ALL = ROW + COL
PLANE = ("y1", "y0", "core", "z1", "z0")
CHIPS = ("xh", "y1", "y0", "z1", "z0", "xl")


def permutation(move):
    pairs = []
    for row in range(16):
        for col in range(8):
            at = (row // 8, row // 2 % 4, row % 2, col // 2, col % 2)
            xh, y, core, z, xl = move(*at)
            pairs.append((row * 8 + col, (xh * 8 + y % 4 * 2 + core) * 8 + z % 4 * 2 + xl))
    return pairs


def exchange(x, axes):
    return lax.all_to_all(x, axes, split_axis=0, concat_axis=0, tiled=True)


def dot_t(a, b):
    return lax.dot_general(a, b, (((1,), (1,)), ((), ())), preferred_element_type=f32)


def split2(x):
    high = x.astype(bf16)
    return high, (x - high.astype(f32)).astype(bf16)


def split3(x):
    high = x.astype(bf16)
    rest = x - high.astype(f32)
    mid = rest.astype(bf16)
    return high, mid, (rest - mid.astype(f32)).astype(bf16)


def solve_t(x, inv_high, inv_low):
    high, low = split2(x)
    return dot_t(high, inv_high) + (dot_t(high, inv_low) + dot_t(low, inv_high))


def pack_kernel(s_ref, x_ref, out_ref, *strip_refs):
    count = 5 if strip_refs else 4
    rows = lax.broadcasted_iota(i32, (32 * count, T), 0)
    cols = lax.broadcasted_iota(i32, (32 * count, T), 1)
    tile = sum(jnp.where(rows // 32 == z, s_ref[16 + z], 0) for z in range(4))
    pick = jnp.where((rows % 32) * 8 + tile == cols, 1.0, 0.0).astype(bf16)
    for g in range(8):
        part = x_ref[0, g * T : (g + 1) * T, :]
        tiles = jnp.dot(pick, part, preferred_element_type=f32).astype(bf16)
        for z in range(4):
            out_ref[0, z, g * 32 : (g + 1) * 32, :] = tiles[z * 32 : (z + 1) * 32]
        if strip_refs:
            strip_refs[0][0, g] = tiles[128:]
    if strip_refs:

        @pl.when(pl.program_id(0) == 0)
        def _():
            strip_refs[1][...] = strip_refs[0][0]


def pack(scalars, tiles, with_strip):
    shapes = [(8, 4, T, T), (16, 8, 32, T), (8, 32, T)]
    specs = [
        pl.BlockSpec((1, 4, T, T), lambda a, s: (s[a], 0, 0, 0)),
        pl.BlockSpec((1, 8, 32, T), lambda a, s: (s[8 + a], 0, 0, 0)),
        pl.BlockSpec((8, 32, T), lambda a, s: (0, 0, 0)),
    ]
    count = 3 if with_strip else 1
    return pl.pallas_call(
        pack_kernel,
        out_shape=[jax.ShapeDtypeStruct(shape, bf16) for shape in shapes[:count]],
        grid_spec=pltpu.PrefetchScalarGridSpec(
            num_scalar_prefetch=1,
            grid=(8,),
            in_specs=[pl.BlockSpec((1, 8 * T, T), lambda a, s: (a, 0, 0))],
            out_specs=specs[:count],
        ),
        compiler_params=pltpu.CompilerParams(vmem_limit_bytes=VMEM),
        cost_estimate=pl.CostEstimate(flops=2 * 64 * T**3, bytes_accessed=1 << 24, transcendentals=0),
        name="pack",
    )(scalars, tiles)


def copy_kernel(s_ref, *refs):
    half = len(refs) // 2
    for x_ref, out_ref in zip(refs[:half], refs[half:]):
        out_ref[...] = x_ref[...]


def compact(lists, tiles):
    count = lists[0].shape[0]
    block = lambda n: pl.BlockSpec((1, 4, T, T), lambda a, s: (s[n * count + a], 0, 0, 0))
    return pl.pallas_call(
        copy_kernel,
        out_shape=[jax.ShapeDtypeStruct((count, 4, T, T), bf16) for _ in lists],
        grid_spec=pltpu.PrefetchScalarGridSpec(
            num_scalar_prefetch=1,
            grid=(count,),
            in_specs=[block(n) for n in range(len(lists))],
            out_specs=[pl.BlockSpec((1, 4, T, T), lambda a, s: (a, 0, 0, 0)) for _ in lists],
        ),
        compiler_params=pltpu.CompilerParams(vmem_limit_bytes=VMEM),
        cost_estimate=pl.CostEstimate(flops=0, bytes_accessed=len(lists) * count << 20, transcendentals=0),
        name="compact",
    )(jnp.concatenate(lists), *[tiles for _ in lists])


def factor_tile(aug):
    row_id = lax.broadcasted_iota(i32, (8, 128), 0)
    groups = NB // 8

    def block(step, _):
        at = pl.multiple_of(step * NB, NB)
        rows = [aug[pl.ds(pl.multiple_of(at + 8 * g, 8), 8), :] for g in range(groups)]
        back = lax.rem(T - at, T)
        diag = [pltpu.roll(rows[g][:, :T], back, 1)[:, :128] for g in range(groups)]
        scales = []
        for s in range(groups):
            cols = [
                [jnp.broadcast_to(diag[g][:, 8 * s + m : 8 * s + m + 1], (8, 128)) for g in range(s, groups)]
                for m in range(8)
            ]
            scale = jnp.zeros((8, 128), f32)
            for m in range(8):
                pivot = jnp.broadcast_to(cols[m][0][m : m + 1, :], (8, 128))
                inverse = 1.0 / pivot
                scale = jnp.where(row_id == m, lax.rsqrt(pivot), scale)
                factor = [c * inverse for c in cols[m]]
                factor[0] = jnp.where(row_id > m, factor[0], 0.0)
                for later in range(m + 1, 8):
                    value = jnp.broadcast_to(cols[later][0][m : m + 1, :], (8, 128))
                    cols[later] = [c - f * value for c, f in zip(cols[later], factor)]
                diag_row = jnp.broadcast_to(diag[s][m : m + 1, :], (8, 128))
                full_row = rows[s][m : m + 1, :]
                for g in range(s, groups):
                    f = factor[g - s]
                    diag[g] = diag[g] - f * diag_row
                    rows[g] = rows[g] - jnp.concatenate([f] * 4, axis=1) * full_row
            scales.append(scale)
        upper = jnp.concatenate(
            [rows[g] * jnp.concatenate([scales[g]] * 4, axis=1) for g in range(groups)], axis=0
        )
        aug[pl.ds(at, NB), :] = upper
        high, mid, low = split3(upper)
        keep = lax.broadcasted_iota(i32, (NB, T), 1) >= at + NB
        none = jnp.zeros((NB, T), bf16)
        lh, lm, ll = [jnp.where(keep, part[:, :T], none) for part in (high, mid, low)]
        left = jnp.concatenate([lh, lh, lm, lh, ll, lm], axis=0)
        right = jnp.concatenate([high, mid, high, low, high, mid], axis=0)
        aug[...] = aug[...] - lax.dot_general(
            left, right, (((0,), (0,)), ((), ())), preferred_element_type=f32
        )
        return 0

    lax.fori_loop(0, T // NB, block, 0)


def pivot_kernel(core_ref, own_ref, other_ref, shift_ref, lb_ref, high_ref, low_ref, work, aug):
    rows = lax.broadcasted_iota(i32, (T, T), 0)
    cols = lax.broadcasted_iota(i32, (T, T), 1)
    core = core_ref[0]
    for t in range(PANELS):
        for u in range(t + 1):
            for s in range(8):
                at = (((s // 2) * 2 + t // 2) * 2 + s % 2) * 4 + u
                part = jnp.where(core == t % 2, own_ref[at].astype(f32), other_ref[at].astype(f32))
                work[t, u, s * 32 : (s + 1) * 32, :] = part
        tile = jnp.where(rows >= cols, work[t, t], 0.0)
        work[t, t] = tile + jnp.where(rows == cols, 0.0, tile).T + jnp.where(rows == cols, shift_ref[t], 0.0)
    for k in range(PANELS):
        aug[:, :T] = work[k, k]
        aug[:, T:] = jnp.where(rows == cols, 1.0, 0.0)
        factor_tile(aug)
        lower = jnp.where(rows >= cols, aug[:, :T].T, 0.0)
        inv_high, inv_low = split2(aug[:, T:])
        high_ref[k] = inv_high
        low_ref[k] = inv_low
        for t in range(k):
            lb_ref[k, t * T : (t + 1) * T, :] = jnp.zeros((T, T), bf16)
        lb_ref[k, k * T : (k + 1) * T, :] = lower.astype(bf16)
        for t in range(k + 1, PANELS):
            lb_ref[k, t * T : (t + 1) * T, :] = solve_t(work[t, k], inv_high, inv_low).astype(bf16)
        for t in range(k + 1, PANELS):
            for u in range(k + 1, t + 1):
                work[t, u] = work[t, u] - dot_t(
                    lb_ref[k, t * T : (t + 1) * T, :], lb_ref[k, u * T : (u + 1) * T, :]
                )


def pivot(core, own, other, shift):
    vmem = pl.BlockSpec(memory_space=pltpu.VMEM)
    return pl.pallas_call(
        pivot_kernel,
        out_shape=(
            jax.ShapeDtypeStruct((PANELS, PANELS * T, T), bf16),
            jax.ShapeDtypeStruct((PANELS, T, T), bf16),
            jax.ShapeDtypeStruct((PANELS, T, T), bf16),
        ),
        in_specs=[pl.BlockSpec(memory_space=pltpu.SMEM), vmem, vmem, vmem],
        out_specs=[vmem] * 3,
        scratch_shapes=[pltpu.VMEM((PANELS, PANELS, T, T), f32), pltpu.VMEM((T, 2 * T), f32)],
        compiler_params=pltpu.CompilerParams(vmem_limit_bytes=VMEM),
        cost_estimate=pl.CostEstimate(flops=45_000_000_000, bytes_accessed=1 << 22, transcendentals=0),
        name="pivot_factor",
    )(core, own, other, shift)


PIECES = ((0, 4), (4, 7))


def panel_kernel(s_ref, *refs):
    strips, (coupling_ref, lb_ref, high_ref, low_ref) = refs[:2], refs[2:6]
    *outs, all_ref, done, block = refs[6:]
    k = pl.program_id(0)
    row, col = s_ref[14], s_ref[15]
    for a in range(RL):
        q = s_ref[a]
        for d in range(8):
            at = pl.ds(pl.multiple_of(a * T + (col ^ d) * 32, 32), 32)
            held = jnp.where(s_ref[7 + a] == 1, strips[d % 2][d // 2, q, 0].astype(f32), 0.0)
            block[at, :] = held
        at = slice(a * T, (a + 1) * T)
        block[at, :] = block[at, :] + coupling_ref[a].astype(f32)
    for j in range(PANELS - 1):

        @pl.when(j < k)
        def _():
            block[...] = block[...] - dot_t(done[j], lb_ref[j, pl.ds(pl.multiple_of(k * T, T), T), :])

    solved = solve_t(block[...], high_ref[k], low_ref[k]).astype(bf16)
    done[k] = solved
    all_ref[...] = solved.reshape(RL, T, T)
    for j, (lo, hi) in enumerate(PIECES):
        outs[j][...] = solved[lo * T : hi * T].reshape(hi - lo, T, T)

    @pl.when(row < PANELS)
    def _():
        pivot_rows = lb_ref[k, pl.ds(pl.multiple_of(jnp.minimum(row, PANELS - 1) * T, T), T), :]
        outs[0][0] = pivot_rows
        all_ref[0] = pivot_rows


def panel_rows(scalars, strips, coupling, lb, high, low):
    whole = lambda shape: pl.BlockSpec(shape, lambda k, s: (0,) * len(shape))
    return pl.pallas_call(
        panel_kernel,
        out_shape=[jax.ShapeDtypeStruct((hi - lo, T, PANELS * T), bf16) for lo, hi in (*PIECES, (0, RL))],
        grid_spec=pltpu.PrefetchScalarGridSpec(
            num_scalar_prefetch=1,
            grid=(PANELS,),
            in_specs=[pl.BlockSpec((4, 8, 1, 32, T), lambda k, s: (0, 0, k, 0, 0))] * 2
            + [
                pl.BlockSpec((RL, T, T), lambda k, s: (0, 0, k)),
                whole((PANELS, PANELS * T, T)),
                whole((PANELS, T, T)),
                whole((PANELS, T, T)),
            ],
            out_specs=[pl.BlockSpec((hi - lo, T, T), lambda k, s: (0, 0, k)) for lo, hi in (*PIECES, (0, RL))],
            scratch_shapes=[pltpu.VMEM((PANELS, RL * T, T), bf16), pltpu.VMEM((RL * T, T), f32)],
        ),
        compiler_params=pltpu.CompilerParams(vmem_limit_bytes=VMEM),
        cost_estimate=pl.CostEstimate(flops=8_000_000_000, bytes_accessed=12 << 20, transcendentals=0),
        name="panel_rows",
    )(scalars, *strips, coupling, lb, high, low)


def front_kernel(s_ref, rows_ref, *refs):
    blocks = refs[0:4]
    count = len(PIECES)
    own, other, out_ref = refs[4 : 4 + count], refs[4 + count : 4 + 2 * count], refs[-1]
    a = pl.program_id(0)
    row, col, core = s_ref[119], s_ref[120], s_ref[121]
    row_ok = [s_ref[21 + a], s_ref[28 + a]]
    mine = rows_ref[0]
    for j, (lo, hi) in enumerate(PIECES):
        for held, parity in ((own[j], core), (other[j], 1 - core)):
            for n in range(hi - lo):
                b = 2 * (lo + n) + parity
                tile = -dot_t(mine, held[n])
                for f in range(2):
                    base = 35 + 42 * f
                    z, e = s_ref[base + b], s_ref[base + 14 + b]
                    ok = row_ok[f] * s_ref[base + 28 + b]
                    near, far = blocks[2 * f][0, z].astype(f32), blocks[2 * f + 1][0, z].astype(f32)
                    tile = tile + jnp.where(e == 0, near, far) * ok.astype(f32)
                out_ref[0, b] = tile.astype(bf16)

    @pl.when((a == 0) & (row < PANELS))
    def _():
        out_ref[...] = jnp.zeros_like(out_ref)

    @pl.when(col < PANELS)
    def _():
        out_ref[0, 0] = rows_ref[0, :, pl.ds(pl.multiple_of(jnp.minimum(col, PANELS - 1) * T, T), T)]


def front(scalars, rows, blocks, own, other):
    block = lambda first: pl.BlockSpec((1, 4, T, T), lambda a, s: (s[first + a], 0, 0, 0))
    whole = lambda x: pl.BlockSpec(x.shape, lambda a, s: (0, 0, 0))
    return pl.pallas_call(
        front_kernel,
        out_shape=jax.ShapeDtypeStruct((RL, CL, T, T), bf16),
        grid_spec=pltpu.PrefetchScalarGridSpec(
            num_scalar_prefetch=1,
            grid=(RL,),
            in_specs=[
                pl.BlockSpec((1, T, PANELS * T), lambda a, s: (a, 0, 0)),
                block(0),
                block(7),
                block(14),
                block(14),
            ]
            + [whole(x) for x in own]
            + [whole(x) for x in other],
            out_specs=pl.BlockSpec((1, CL, T, T), lambda a, s: (a, 0, 0, 0)),
        ),
        compiler_params=pltpu.CompilerParams(vmem_limit_bytes=VMEM),
        cost_estimate=pl.CostEstimate(
            flops=2 * RL * CL * T * T * PANELS * T, bytes_accessed=40 << 20, transcendentals=0
        ),
        name="front",
    )(scalars, rows, *blocks, *own, *other)


def per_device(children, child_maps, coupling, pivot_shift):
    row, col = lax.axis_index(ROW), lax.axis_index(COL)
    xh, core, xl = lax.axis_index("xh"), lax.axis_index("core"), lax.axis_index("xl")
    rho = row % 8
    eight = jnp.arange(8)

    own_map = child_maps[xh].reshape(8, 8)
    row_to = jnp.sum(jnp.where(eight[None, :] == rho, own_map, 0), axis=1)
    col_to = jnp.sum(jnp.where(eight[None, :] == col, own_map, 0), axis=1)
    by_to = lambda slots: jnp.sum(jnp.where(col_to[None, :] % 8 == slots[:, None], eight[None, :], 0), axis=1)
    same_to = 2 * jnp.arange(4) + xl
    pack_scalars = lambda to: jnp.concatenate([row_to % 8, row_to % 16, by_to(to)]).astype(i32)

    both = jnp.stack([child_maps[xh], child_maps[1 - xh]])
    at = jnp.arange(64)
    row_is = both[:, None, :] == (row + 16 * jnp.arange(RL))[None, :, None]
    row_t = jnp.sum(jnp.where(row_is, at, 0), axis=2)
    row_ok = jnp.any(row_is, axis=2).astype(i32)
    col_is = both[:, None, :] == (col + 8 * jnp.arange(CL))[None, :, None]
    col_u = jnp.sum(jnp.where(col_is, at, 0), axis=2)
    col_ok = jnp.any(col_is, axis=2).astype(i32)
    by_q = both.reshape(2, 8, 8)
    half = jnp.sum(jnp.where(by_q % 8 == rho, by_q // 8 % 2, 0), axis=1)
    rank_of = lambda hit: jnp.sum(
        jnp.where(eight[None, :] < eight[:, None], hit[..., None, :].astype(i32), 0), axis=-1
    )
    rank = rank_of(half == xh)
    slot = jnp.sum(jnp.where(row_t[:, :, None] % 8 == eight, rank[:, None, :], 0), axis=2) * row_ok

    def chosen(hit):
        order = jnp.where(hit[None, :] & (rank_of(hit)[None, :] == jnp.arange(K)[:, None]), eight[None, :], 0)
        return jnp.sum(order, axis=1).astype(i32)

    to_own, to_other = chosen(half[0] == xh), chosen(half[0] != xh)

    zero_is = child_maps[0][None, :] == (row + 16 * jnp.arange(RL))[:, None]
    panel_scalars = jnp.concatenate(
        [
            jnp.sum(jnp.where(zero_is, at % 8, 0), axis=1),
            jnp.any(zero_is, axis=1).astype(i32),
            row.reshape(1),
            col.reshape(1),
        ]
    ).astype(i32)
    front_scalars = jnp.concatenate(
        [row_t[0] % 8, slot[0], slot[1], row_ok[0], row_ok[1]]
        + [x[f] for f in range(2) for x in (col_u % 8 // 2, (col_u % 2) ^ xl, col_ok)]
        + [row.reshape(1), col.reshape(1), core.reshape(1)]
    ).astype(i32)

    tiles = children.reshape(8, 8 * T, T)
    (cross,) = pack(pack_scalars(same_to ^ 1), tiles, False)
    same, strip, first = pack(pack_scalars(same_to), tiles, True)

    move = lambda f, e: permutation(lambda xh, y, core, z, xl: (xh ^ f, y, core, z, xl ^ e))
    swap = permutation(lambda xh, y, core, z, xl: (xh, y, 1 - core, z, xl))
    flip = lambda d: permutation(lambda xh, y, core, z, xl: (xh, y, core, z ^ (d // 2), xl ^ (d % 2)))
    cross = exchange(cross.reshape(32, T, T), PLANE).reshape(8, 4, T, T)
    strip, cross = lax.optimization_barrier((strip, cross))

    strip = exchange(strip.reshape(128, 32, T), ALL)
    send_01, send_11 = compact((to_own[:FIRST], to_other[:FIRST]), cross)

    piece = first[0]
    for s in range(1, 8):
        pairs = []
        for owner in range(16):
            t, u = owner // 4, owner % 4
            pairs.append((t * 8 + u, (t + s // 2 * 4) * 8 + u + s % 2 * 4))
        arrived = lax.ppermute(first[s], ALL, pairs)
        piece = jnp.where(row // 4 * 2 + col // 4 == s, arrived, piece)
    mine = strip.reshape(16, 8, 32, T)[:8, :PANELS]
    held = [mine] + [lax.ppermute(mine, ALL, flip(2 * d)) for d in range(1, 4)]
    piece, held, send_01, send_11 = lax.optimization_barrier((piece, held, send_01, send_11))
    own_half = exchange(jnp.broadcast_to(piece[None], (64, 32, T)), CHIPS)
    other_half = lax.ppermute(own_half, ALL, swap)
    same, held, other_half, send_01, send_11 = lax.optimization_barrier(
        (same, held, other_half, send_01, send_11)
    )

    held = jnp.stack(held)
    strips = [held, lax.ppermute(held, ALL, flip(1))]
    from_01 = lax.ppermute(send_01, ALL, move(0, 1))
    from_11 = lax.ppermute(send_11, ALL, move(1, 1))
    same = exchange(same.reshape(32, T, T), PLANE).reshape(8, 4, T, T)

    lb, high, low = pivot(core.reshape(1), own_half, other_half, pivot_shift.reshape(PANELS, T, 1))
    *rows, all_rows = panel_rows(panel_scalars, strips, coupling.reshape(RL, T, PANELS * T), lb, high, low)

    own, other = [], []
    for j in range(len(PIECES)):
        turn = permutation(
            lambda xh, y, core, z, xl: (xl ^ core ^ xh, z - y + 2 * j + core + 2 * xh, xh, y, core)
        )
        own.append(lax.ppermute(rows[j], ALL, turn))
        other.append(lax.ppermute(own[-1], ALL, swap))

    same, from_01, from_11, all_rows = lax.optimization_barrier((same, from_01, from_11, all_rows))
    from_10 = lax.ppermute(compact((to_other[:FIRST],), same)[0], ALL, move(1, 0))

    def finish(f01, f10, f11):
        return front(front_scalars, all_rows, (same, f01, f10, f11), own, other)

    def finish_rest(f01, f10, f11):
        rest_01, rest_11 = compact((to_own[FIRST:], to_other[FIRST:]), cross)
        rest_10 = compact((to_other[FIRST:],), same)[0]
        rest_01 = lax.ppermute(rest_01, ALL, move(0, 1))
        rest_11 = lax.ppermute(rest_11, ALL, move(1, 1))
        rest_10 = lax.ppermute(rest_10, ALL, move(1, 0))
        joined = [jnp.concatenate(pair) for pair in ((f01, rest_01), (f10, rest_10), (f11, rest_11))]
        return finish(*joined)

    ones = child_maps[:, None, :] % 16 == jnp.arange(16)[None, :, None]
    most = jnp.max(jnp.sum(ones.astype(i32), axis=2))
    result = lax.cond(most <= FIRST, finish, finish_rest, from_01, from_10, from_11)
    return jnp.transpose(result, (0, 2, 1, 3)).reshape(RL, 1, T, CL, 1, T)


def solution(mesh):
    fine = Mesh(mesh.devices.reshape((2,) * 7), ALL)
    in_specs = (P(None, ROW, None, None, COL, None), P(), P(None, ROW, None, None), P())
    out_specs = P(None, ROW, None, None, COL, None)
    return jax.shard_map(per_device, mesh=fine, in_specs=in_specs, out_specs=out_specs, check_vma=False)
```

```python
import jax
import jax.numpy as jnp
from jax import lax
from jax.experimental import pallas as pl
from jax.experimental.pallas import tpu as pltpu
from jax.sharding import Mesh, PartitionSpec as P

f32 = jnp.float32
bf16 = jnp.bfloat16
i32 = jnp.int32

T = 256
PANELS = 4
NB = 32
RL, CL = 7, 14
K = 7
FIRST = 5
VMEM = 56 * 1024 * 1024

ROW = ("xh", "y1", "y0", "core")
COL = ("z1", "z0", "xl")
ALL = ROW + COL
PLANE = ("y1", "y0", "core", "z1", "z0")
CHIPS = ("xh", "y1", "y0", "z1", "z0", "xl")


def permutation(move):
    pairs = []
    for row in range(16):
        for col in range(8):
            at = (row // 8, row // 2 % 4, row % 2, col // 2, col % 2)
            xh, y, core, z, xl = move(*at)
            pairs.append((row * 8 + col, (xh * 8 + y % 4 * 2 + core) * 8 + z % 4 * 2 + xl))
    return pairs


def exchange(x, axes):
    return lax.all_to_all(x, axes, split_axis=0, concat_axis=0, tiled=True)


def dot_t(a, b):
    return lax.dot_general(a, b, (((1,), (1,)), ((), ())), preferred_element_type=f32)


def split2(x):
    high = x.astype(bf16)
    return high, (x - high.astype(f32)).astype(bf16)


def split3(x):
    high = x.astype(bf16)
    rest = x - high.astype(f32)
    mid = rest.astype(bf16)
    return high, mid, (rest - mid.astype(f32)).astype(bf16)


def solve_t(x, inv_high, inv_low):
    high, low = split2(x)
    return dot_t(high, inv_high) + (dot_t(high, inv_low) + dot_t(low, inv_high))


def pack_kernel(s_ref, x_ref, out_ref, *strip_refs):
    count = 5 if strip_refs else 4
    rows = lax.broadcasted_iota(i32, (32 * count, T), 0)
    cols = lax.broadcasted_iota(i32, (32 * count, T), 1)
    tile = sum(jnp.where(rows // 32 == z, s_ref[16 + z], 0) for z in range(4))
    pick = jnp.where((rows % 32) * 8 + tile == cols, 1.0, 0.0).astype(bf16)
    for g in range(8):
        part = x_ref[0, g * T : (g + 1) * T, :]
        tiles = jnp.dot(pick, part, preferred_element_type=f32).astype(bf16)
        for z in range(4):
            out_ref[0, z, g * 32 : (g + 1) * 32, :] = tiles[z * 32 : (z + 1) * 32]
        if strip_refs:
            strip_refs[0][0, g] = tiles[128:]
    if strip_refs:

        @pl.when(pl.program_id(0) == 0)
        def _():
            strip_refs[1][...] = strip_refs[0][0]


def pack(scalars, tiles, with_strip):
    shapes = [(8, 4, T, T), (16, 8, 32, T), (8, 32, T)]
    specs = [
        pl.BlockSpec((1, 4, T, T), lambda a, s: (s[a], 0, 0, 0)),
        pl.BlockSpec((1, 8, 32, T), lambda a, s: (s[8 + a], 0, 0, 0)),
        pl.BlockSpec((8, 32, T), lambda a, s: (0, 0, 0)),
    ]
    count = 3 if with_strip else 1
    return pl.pallas_call(
        pack_kernel,
        out_shape=[jax.ShapeDtypeStruct(shape, bf16) for shape in shapes[:count]],
        grid_spec=pltpu.PrefetchScalarGridSpec(
            num_scalar_prefetch=1,
            grid=(8,),
            in_specs=[pl.BlockSpec((1, 8 * T, T), lambda a, s: (a, 0, 0))],
            out_specs=specs[:count],
        ),
        compiler_params=pltpu.CompilerParams(vmem_limit_bytes=VMEM),
        cost_estimate=pl.CostEstimate(flops=2 * 64 * T**3, bytes_accessed=1 << 24, transcendentals=0),
        name="pack",
    )(scalars, tiles)


def copy_kernel(s_ref, *refs):
    half = len(refs) // 2
    for x_ref, out_ref in zip(refs[:half], refs[half:]):
        out_ref[...] = x_ref[...]


def compact(lists, tiles):
    count = lists[0].shape[0]
    block = lambda n: pl.BlockSpec((1, 4, T, T), lambda a, s: (s[n * count + a], 0, 0, 0))
    return pl.pallas_call(
        copy_kernel,
        out_shape=[jax.ShapeDtypeStruct((count, 4, T, T), bf16) for _ in lists],
        grid_spec=pltpu.PrefetchScalarGridSpec(
            num_scalar_prefetch=1,
            grid=(count,),
            in_specs=[block(n) for n in range(len(lists))],
            out_specs=[pl.BlockSpec((1, 4, T, T), lambda a, s: (a, 0, 0, 0)) for _ in lists],
        ),
        compiler_params=pltpu.CompilerParams(vmem_limit_bytes=VMEM),
        cost_estimate=pl.CostEstimate(flops=0, bytes_accessed=len(lists) * count << 20, transcendentals=0),
        name="compact",
    )(jnp.concatenate(lists), *[tiles for _ in lists])


def factor_tile(aug):
    row_id = lax.broadcasted_iota(i32, (8, 128), 0)
    groups = NB // 8

    def block(step, _):
        at = pl.multiple_of(step * NB, NB)
        rows = [aug[pl.ds(pl.multiple_of(at + 8 * g, 8), 8), :] for g in range(groups)]
        back = lax.rem(T - at, T)
        diag = [pltpu.roll(rows[g][:, :T], back, 1)[:, :128] for g in range(groups)]
        scales = []
        for s in range(groups):
            cols = [
                [jnp.broadcast_to(diag[g][:, 8 * s + m : 8 * s + m + 1], (8, 128)) for g in range(s, groups)]
                for m in range(8)
            ]
            scale = jnp.zeros((8, 128), f32)
            for m in range(8):
                pivot = jnp.broadcast_to(cols[m][0][m : m + 1, :], (8, 128))
                inverse = 1.0 / pivot
                scale = jnp.where(row_id == m, lax.rsqrt(pivot), scale)
                factor = [c * inverse for c in cols[m]]
                factor[0] = jnp.where(row_id > m, factor[0], 0.0)
                for later in range(m + 1, 8):
                    value = jnp.broadcast_to(cols[later][0][m : m + 1, :], (8, 128))
                    cols[later] = [c - f * value for c, f in zip(cols[later], factor)]
                diag_row = jnp.broadcast_to(diag[s][m : m + 1, :], (8, 128))
                full_row = rows[s][m : m + 1, :]
                for g in range(s, groups):
                    f = factor[g - s]
                    diag[g] = diag[g] - f * diag_row
                    rows[g] = rows[g] - jnp.concatenate([f] * 4, axis=1) * full_row
            scales.append(scale)
        upper = jnp.concatenate(
            [rows[g] * jnp.concatenate([scales[g]] * 4, axis=1) for g in range(groups)], axis=0
        )
        aug[pl.ds(at, NB), :] = upper
        high, mid, low = split3(upper)
        keep = lax.broadcasted_iota(i32, (NB, T), 1) >= at + NB
        none = jnp.zeros((NB, T), bf16)
        lh, lm, ll = [jnp.where(keep, part[:, :T], none) for part in (high, mid, low)]
        left = jnp.concatenate([lh, lh, lm, lh, ll, lm], axis=0)
        right = jnp.concatenate([high, mid, high, low, high, mid], axis=0)
        aug[...] = aug[...] - lax.dot_general(
            left, right, (((0,), (0,)), ((), ())), preferred_element_type=f32
        )
        return 0

    lax.fori_loop(0, T // NB, block, 0)


def pivot_kernel(core_ref, own_ref, other_ref, shift_ref, lb_ref, high_ref, low_ref, work, aug):
    rows = lax.broadcasted_iota(i32, (T, T), 0)
    cols = lax.broadcasted_iota(i32, (T, T), 1)
    core = core_ref[0]
    for t in range(PANELS):
        for u in range(t + 1):
            for s in range(8):
                at = (((s // 2) * 2 + t // 2) * 2 + s % 2) * 4 + u
                part = jnp.where(core == t % 2, own_ref[at].astype(f32), other_ref[at].astype(f32))
                work[t, u, s * 32 : (s + 1) * 32, :] = part
        tile = jnp.where(rows >= cols, work[t, t], 0.0)
        work[t, t] = tile + jnp.where(rows == cols, 0.0, tile).T + jnp.where(rows == cols, shift_ref[t], 0.0)
    for k in range(PANELS):
        aug[:, :T] = work[k, k]
        aug[:, T:] = jnp.where(rows == cols, 1.0, 0.0)
        factor_tile(aug)
        lower = jnp.where(rows >= cols, aug[:, :T].T, 0.0)
        inv_high, inv_low = split2(aug[:, T:])
        high_ref[k] = inv_high
        low_ref[k] = inv_low
        for t in range(k):
            lb_ref[k, t * T : (t + 1) * T, :] = jnp.zeros((T, T), bf16)
        lb_ref[k, k * T : (k + 1) * T, :] = lower.astype(bf16)
        for t in range(k + 1, PANELS):
            lb_ref[k, t * T : (t + 1) * T, :] = solve_t(work[t, k], inv_high, inv_low).astype(bf16)
        for t in range(k + 1, PANELS):
            for u in range(k + 1, t + 1):
                work[t, u] = work[t, u] - dot_t(
                    lb_ref[k, t * T : (t + 1) * T, :], lb_ref[k, u * T : (u + 1) * T, :]
                )


def pivot(core, own, other, shift):
    vmem = pl.BlockSpec(memory_space=pltpu.VMEM)
    return pl.pallas_call(
        pivot_kernel,
        out_shape=(
            jax.ShapeDtypeStruct((PANELS, PANELS * T, T), bf16),
            jax.ShapeDtypeStruct((PANELS, T, T), bf16),
            jax.ShapeDtypeStruct((PANELS, T, T), bf16),
        ),
        in_specs=[pl.BlockSpec(memory_space=pltpu.SMEM), vmem, vmem, vmem],
        out_specs=[vmem] * 3,
        scratch_shapes=[pltpu.VMEM((PANELS, PANELS, T, T), f32), pltpu.VMEM((T, 2 * T), f32)],
        compiler_params=pltpu.CompilerParams(vmem_limit_bytes=VMEM),
        cost_estimate=pl.CostEstimate(flops=45_000_000_000, bytes_accessed=1 << 22, transcendentals=0),
        name="pivot_factor",
    )(core, own, other, shift)


PIECES = ((0, 4), (4, 7))


def panel_kernel(s_ref, *refs):
    strips, (coupling_ref, lb_ref, high_ref, low_ref) = refs[:2], refs[2:6]
    *outs, all_ref, done, block = refs[6:]
    k = pl.program_id(0)
    row, col = s_ref[14], s_ref[15]
    for a in range(RL):
        q = s_ref[a]
        for d in range(8):
            at = pl.ds(pl.multiple_of(a * T + (col ^ d) * 32, 32), 32)
            held = jnp.where(s_ref[7 + a] == 1, strips[d % 2][d // 2, q, 0].astype(f32), 0.0)
            block[at, :] = held
        at = slice(a * T, (a + 1) * T)
        block[at, :] = block[at, :] + coupling_ref[a].astype(f32)
    for j in range(PANELS - 1):

        @pl.when(j < k)
        def _():
            block[...] = block[...] - dot_t(done[j], lb_ref[j, pl.ds(pl.multiple_of(k * T, T), T), :])

    solved = solve_t(block[...], high_ref[k], low_ref[k]).astype(bf16)
    done[k] = solved
    all_ref[...] = solved.reshape(RL, T, T)
    for j, (lo, hi) in enumerate(PIECES):
        outs[j][...] = solved[lo * T : hi * T].reshape(hi - lo, T, T)

    @pl.when(row < PANELS)
    def _():
        pivot_rows = lb_ref[k, pl.ds(pl.multiple_of(jnp.minimum(row, PANELS - 1) * T, T), T), :]
        outs[0][0] = pivot_rows
        all_ref[0] = pivot_rows


def panel_rows(scalars, strips, coupling, lb, high, low):
    whole = lambda shape: pl.BlockSpec(shape, lambda k, s: (0,) * len(shape))
    return pl.pallas_call(
        panel_kernel,
        out_shape=[jax.ShapeDtypeStruct((hi - lo, T, PANELS * T), bf16) for lo, hi in (*PIECES, (0, RL))],
        grid_spec=pltpu.PrefetchScalarGridSpec(
            num_scalar_prefetch=1,
            grid=(PANELS,),
            in_specs=[pl.BlockSpec((4, 8, 1, 32, T), lambda k, s: (0, 0, k, 0, 0))] * 2
            + [
                pl.BlockSpec((RL, T, T), lambda k, s: (0, 0, k)),
                whole((PANELS, PANELS * T, T)),
                whole((PANELS, T, T)),
                whole((PANELS, T, T)),
            ],
            out_specs=[pl.BlockSpec((hi - lo, T, T), lambda k, s: (0, 0, k)) for lo, hi in (*PIECES, (0, RL))],
            scratch_shapes=[pltpu.VMEM((PANELS, RL * T, T), bf16), pltpu.VMEM((RL * T, T), f32)],
        ),
        compiler_params=pltpu.CompilerParams(vmem_limit_bytes=VMEM),
        cost_estimate=pl.CostEstimate(flops=8_000_000_000, bytes_accessed=12 << 20, transcendentals=0),
        name="panel_rows",
    )(scalars, *strips, coupling, lb, high, low)


def front_kernel(s_ref, rows_ref, *refs):
    blocks = refs[0:4]
    count = len(PIECES)
    own, other, out_ref = refs[4 : 4 + count], refs[4 + count : 4 + 2 * count], refs[-1]
    a = pl.program_id(0)
    row, col, core = s_ref[119], s_ref[120], s_ref[121]
    row_ok = [s_ref[21 + a], s_ref[28 + a]]
    mine = rows_ref[0]
    for j, (lo, hi) in enumerate(PIECES):
        for held, parity in ((own[j], core), (other[j], 1 - core)):
            for n in range(hi - lo):
                b = 2 * (lo + n) + parity
                tile = -dot_t(mine, held[n])
                for f in range(2):
                    base = 35 + 42 * f
                    z, e = s_ref[base + b], s_ref[base + 14 + b]
                    ok = row_ok[f] * s_ref[base + 28 + b]
                    held_tile = jnp.where(e == 0, blocks[2 * f][0, z], blocks[2 * f + 1][0, z])
                    tile = tile + held_tile.astype(f32) * ok.astype(f32)
                out_ref[0, b] = tile.astype(bf16)

    @pl.when((a == 0) & (row < PANELS))
    def _():
        out_ref[...] = jnp.zeros_like(out_ref)

    @pl.when(col < PANELS)
    def _():
        out_ref[0, 0] = rows_ref[0, :, pl.ds(pl.multiple_of(jnp.minimum(col, PANELS - 1) * T, T), T)]


def front(scalars, rows, blocks, own, other):
    block = lambda first: pl.BlockSpec((1, 4, T, T), lambda a, s: (s[first + a], 0, 0, 0))
    whole = lambda x: pl.BlockSpec(x.shape, lambda a, s: (0, 0, 0))
    return pl.pallas_call(
        front_kernel,
        out_shape=jax.ShapeDtypeStruct((RL, CL, T, T), bf16),
        grid_spec=pltpu.PrefetchScalarGridSpec(
            num_scalar_prefetch=1,
            grid=(RL,),
            in_specs=[
                pl.BlockSpec((1, T, PANELS * T), lambda a, s: (a, 0, 0)),
                block(0),
                block(7),
                block(14),
                block(14),
            ]
            + [whole(x) for x in own]
            + [whole(x) for x in other],
            out_specs=pl.BlockSpec((1, CL, T, T), lambda a, s: (a, 0, 0, 0)),
        ),
        compiler_params=pltpu.CompilerParams(vmem_limit_bytes=VMEM),
        cost_estimate=pl.CostEstimate(
            flops=2 * RL * CL * T * T * PANELS * T, bytes_accessed=40 << 20, transcendentals=0
        ),
        name="front",
    )(scalars, rows, *blocks, *own, *other)


def per_device(children, child_maps, coupling, pivot_shift):
    row, col = lax.axis_index(ROW), lax.axis_index(COL)
    xh, core, xl = lax.axis_index("xh"), lax.axis_index("core"), lax.axis_index("xl")
    rho = row % 8
    eight = jnp.arange(8)

    own_map = child_maps[xh].reshape(8, 8)
    row_to = jnp.sum(jnp.where(eight[None, :] == rho, own_map, 0), axis=1)
    col_to = jnp.sum(jnp.where(eight[None, :] == col, own_map, 0), axis=1)
    by_to = lambda slots: jnp.sum(jnp.where(col_to[None, :] % 8 == slots[:, None], eight[None, :], 0), axis=1)
    same_to = 2 * jnp.arange(4) + xl
    pack_scalars = lambda to: jnp.concatenate([row_to % 8, row_to % 16, by_to(to)]).astype(i32)

    both = jnp.stack([child_maps[xh], child_maps[1 - xh]])
    at = jnp.arange(64)
    row_is = both[:, None, :] == (row + 16 * jnp.arange(RL))[None, :, None]
    row_t = jnp.sum(jnp.where(row_is, at, 0), axis=2)
    row_ok = jnp.any(row_is, axis=2).astype(i32)
    col_is = both[:, None, :] == (col + 8 * jnp.arange(CL))[None, :, None]
    col_u = jnp.sum(jnp.where(col_is, at, 0), axis=2)
    col_ok = jnp.any(col_is, axis=2).astype(i32)
    by_q = both.reshape(2, 8, 8)
    half = jnp.sum(jnp.where(by_q % 8 == rho, by_q // 8 % 2, 0), axis=1)
    rank_of = lambda hit: jnp.sum(
        jnp.where(eight[None, :] < eight[:, None], hit[..., None, :].astype(i32), 0), axis=-1
    )
    rank = rank_of(half == xh)
    slot = jnp.sum(jnp.where(row_t[:, :, None] % 8 == eight, rank[:, None, :], 0), axis=2) * row_ok

    def chosen(hit):
        order = jnp.where(hit[None, :] & (rank_of(hit)[None, :] == jnp.arange(K)[:, None]), eight[None, :], 0)
        return jnp.sum(order, axis=1).astype(i32)

    to_own, to_other = chosen(half[0] == xh), chosen(half[0] != xh)

    zero_is = child_maps[0][None, :] == (row + 16 * jnp.arange(RL))[:, None]
    panel_scalars = jnp.concatenate(
        [
            jnp.sum(jnp.where(zero_is, at % 8, 0), axis=1),
            jnp.any(zero_is, axis=1).astype(i32),
            row.reshape(1),
            col.reshape(1),
        ]
    ).astype(i32)
    front_scalars = jnp.concatenate(
        [row_t[0] % 8, slot[0], slot[1], row_ok[0], row_ok[1]]
        + [x[f] for f in range(2) for x in (col_u % 8 // 2, (col_u % 2) ^ xl, col_ok)]
        + [row.reshape(1), col.reshape(1), core.reshape(1)]
    ).astype(i32)

    tiles = children.reshape(8, 8 * T, T)
    (cross,) = pack(pack_scalars(same_to ^ 1), tiles, False)
    same, strip, first = pack(pack_scalars(same_to), tiles, True)

    move = lambda f, e: permutation(lambda xh, y, core, z, xl: (xh ^ f, y, core, z, xl ^ e))
    swap = permutation(lambda xh, y, core, z, xl: (xh, y, 1 - core, z, xl))
    flip = lambda d: permutation(lambda xh, y, core, z, xl: (xh, y, core, z ^ (d // 2), xl ^ (d % 2)))
    cross = exchange(cross.reshape(32, T, T), PLANE).reshape(8, 4, T, T)
    strip, cross = lax.optimization_barrier((strip, cross))

    strip = exchange(strip.reshape(128, 32, T), ALL)
    send_01, send_11 = compact((to_own[:FIRST], to_other[:FIRST]), cross)

    piece = first[0]
    for s in range(1, 8):
        pairs = []
        for owner in range(16):
            t, u = owner // 4, owner % 4
            pairs.append((t * 8 + u, (t + s // 2 * 4) * 8 + u + s % 2 * 4))
        arrived = lax.ppermute(first[s], ALL, pairs)
        piece = jnp.where(row // 4 * 2 + col // 4 == s, arrived, piece)
    mine = strip.reshape(16, 8, 32, T)[:8, :PANELS]
    held = [mine] + [lax.ppermute(mine, ALL, flip(2 * d)) for d in range(1, 4)]
    piece, held, send_01, send_11 = lax.optimization_barrier((piece, held, send_01, send_11))
    own_half = exchange(jnp.broadcast_to(piece[None], (64, 32, T)), CHIPS)
    other_half = lax.ppermute(own_half, ALL, swap)
    same, held, other_half, send_01, send_11 = lax.optimization_barrier(
        (same, held, other_half, send_01, send_11)
    )

    held = jnp.stack(held)
    strips = [held, lax.ppermute(held, ALL, flip(1))]
    from_01 = lax.ppermute(send_01, ALL, move(0, 1))
    from_11 = lax.ppermute(send_11, ALL, move(1, 1))
    same = exchange(same.reshape(32, T, T), PLANE).reshape(8, 4, T, T)

    lb, high, low = pivot(core.reshape(1), own_half, other_half, pivot_shift.reshape(PANELS, T, 1))
    *rows, all_rows = panel_rows(panel_scalars, strips, coupling.reshape(RL, T, PANELS * T), lb, high, low)

    own, other = [], []
    for j in range(len(PIECES)):
        turn = permutation(
            lambda xh, y, core, z, xl: (xl ^ core ^ xh, z - y + 2 * j + core + 2 * xh, xh, y, core)
        )
        own.append(lax.ppermute(rows[j], ALL, turn))
        other.append(lax.ppermute(own[-1], ALL, swap))

    same, from_01, from_11, all_rows = lax.optimization_barrier((same, from_01, from_11, all_rows))
    from_10 = lax.ppermute(compact((to_other[:FIRST],), same)[0], ALL, move(1, 0))

    def finish(f01, f10, f11):
        return front(front_scalars, all_rows, (same, f01, f10, f11), own, other)

    def finish_rest(f01, f10, f11):
        rest_01, rest_11 = compact((to_own[FIRST:], to_other[FIRST:]), cross)
        rest_10 = compact((to_other[FIRST:],), same)[0]
        rest_01 = lax.ppermute(rest_01, ALL, move(0, 1))
        rest_11 = lax.ppermute(rest_11, ALL, move(1, 1))
        rest_10 = lax.ppermute(rest_10, ALL, move(1, 0))
        joined = [jnp.concatenate(pair) for pair in ((f01, rest_01), (f10, rest_10), (f11, rest_11))]
        return finish(*joined)

    ones = child_maps[:, None, :] % 16 == jnp.arange(16)[None, :, None]
    most = jnp.max(jnp.sum(ones.astype(i32), axis=2))
    result = lax.cond(most <= FIRST, finish, finish_rest, from_01, from_10, from_11)
    return jnp.transpose(result, (0, 2, 1, 3)).reshape(RL, 1, T, CL, 1, T)


def solution(mesh):
    fine = Mesh(mesh.devices.reshape((2,) * 7), ALL)
    in_specs = (P(None, ROW, None, None, COL, None), P(), P(None, ROW, None, None), P())
    out_specs = P(None, ROW, None, None, COL, None)
    return jax.shard_map(per_device, mesh=fine, in_specs=in_specs, out_specs=out_specs, check_vma=False)
```
